32 devices in a mesh: expert: 2 (over x), shard: 4 (over z), dp: 4 (over y, core).
Axes of the slice: x: 2, y: 2, z: 4, core: 2. Of those that a mesh axis runs over, the one named last changes fastest.
Arguments:
- tokens: bfloat16 [4096, 768], P(('expert', 'shard', 'dp')), may hold values from -6 to 6
- lengths: int32 [32, 4], P(('expert', 'shard', 'dp')), may hold values from 1 to 64, 128 in all within a row
- routes: int32 [4096, 1], P(('expert', 'shard', 'dp')), may hold values from 0 to 1
- buckets: int32 [255], replicated, may hold values from 0 to 31
- bias_table: float32 [32, 12], replicated, may hold values from -5 to 5
- projection: bfloat16 [2, 768, 2304], P(None, ('shard', 'dp')), may hold values from -0.21875 to 0.21875
- collector: bfloat16 [2, 768, 768], P(None, ('shard', 'dp')), may hold values from -0.875 to 0.875
- router: bfloat16 [2, 768, 2], P(None, ('shard', 'dp')), may hold values from -0.15625 to 0.15625
- scales: bfloat16 [2, 768, 2], P(None, ('shard', 'dp')), may hold values from 0.099609375 to 1.8984375
- upward: bfloat16 [2, 2, 768, 3072], P(None, 'expert', None, 'shard'), may hold values from -0.21875 to 0.21875
- downward: bfloat16 [2, 2, 3072, 768], P(None, 'expert', 'shard'), may hold values from -0.875 to 0.875
- cotangent: bfloat16 [4096, 768], P(('expert', 'shard', 'dp')), may hold values from -6 to 6
Outputs:
- activations: bfloat16 [4096, 768], P(('expert', 'shard', 'dp'))
- tokens_grad: float32 [4096, 768], P(('expert', 'shard', 'dp'))
- projection_grad: float32 [2, 768, 2304], P(None, ('shard', 'dp'))
- collector_grad: float32 [2, 768, 768], P(None, ('shard', 'dp'))
- router_grad: float32 [2, 768, 2], P(None, ('shard', 'dp'))
- scales_grad: float32 [2, 768, 2], P(None, ('shard', 'dp'))
- upward_grad: float32 [2, 2, 768, 3072], P(None, 'expert', 'dp', 'shard')
- downward_grad: float32 [2, 2, 3072, 768], P(None, 'expert', 'shard', 'dp')
- table_grad: float32 [32, 12], replicated
The draws below stay inside these ranges and needn't reach their ends.
Inputs may be any that keep to these rules, and one draw needn't show every extreme that they name: `lengths`: each row sums to 128; the longest in every row is 64. `routes`: every expert is named by some token.
All inputs are finite; a program needn't handle non-finite values.
Results may differ from the reference program's by a relative error of at most 0.029.
Values may be sent and summed in bfloat16 or wider, within the bound.
A program may use at most 128 MiB of HBM per device.

```python
import math
import jax
import jax.numpy as jnp
import numpy as np
from jax import lax

D = 768
HEADS = 12
HEAD_DIM = 64
FF = 3072
BUCKETS = 32
LAYERS = 2
SEQS_DEV = 4
TOK_DEV = 128
SEQ_MOST = 64
EXPERTS = 2
CAP = 80
TOKENS = 4096
DEVICES = 32


def place_ends(array, rng, least, top_value):
    longest = array.shape.index(max(array.shape))
    spots = []
    for shift in (0, 1):
        where = [jax.random.randint(jax.random.fold_in(rng, axis), (), 0, length) for axis, length in enumerate(array.shape)]
        where[longest] = (where[longest] + shift) % array.shape[longest]
        spots.append(tuple(where))
    return array.at[spots[0]].set(least).at[spots[1]].set(top_value)


def shard_levels(key, shape, shards, low, high):
    def one(axis_at, blocks):
        heights = jax.random.uniform(jax.random.fold_in(jax.random.fold_in(key, 6), axis_at), (blocks,), jnp.float32, low / len(shards), high / len(shards))
        return jnp.repeat(jnp.exp(heights), shape[axis_at] // blocks).reshape((-1,) + (1,) * (len(shape) - axis_at - 1))

    gain = one(*shards[0])
    for cut in shards[1:]:
        gain = gain * one(*cut)
    return gain


def picks_of(own_key, rows, count, top, lift):
    order = jax.random.permutation(jax.random.fold_in(own_key, 1), count)
    boost = order
    for power in range(3):
        boost = boost * boost // count
    boost = boost * lift // count
    chance = jax.random.randint(jax.random.fold_in(own_key, 2), (rows, count), 0, 4096) + boost
    holders = jax.random.permutation(jax.random.fold_in(own_key, 3), rows)[jnp.arange(count) % rows]
    chance = jnp.where(jnp.arange(rows)[:, None] == holders[None, :], 1 << 14, chance)
    merit = chance * count + jnp.arange(count)
    return lax.top_k(merit.astype(jnp.int32), top)[1].astype(jnp.int32)


def profile(amount, total, most, lean):
    loads = [(1 << 20) // math.isqrt(standing ** lean) + 1 for standing in range(2, amount + 1)]
    spare, holding = total - most - (amount - 1), [1] * (amount - 1)
    while spare > 0:
        movable = [i for i in range(amount - 1) if holding[i] < most]
        pool, left = sum([loads[i] for i in movable]), spare
        for i in movable:
            more = min(most - holding[i], max(1, left * loads[i] // pool), spare)
            holding[i] = holding[i] + more
            spare = spare - more
    return np.array([most] + holding)


def uneven(key, count, total, most, slope):
    if count == 2:
        one = jax.random.randint(key, (), max(1, total - most), min(most, total - 1) + 1)
        return jnp.stack([one, total - one])
    sizes = jnp.asarray(profile(count, total, most, slope), jnp.int32)
    pairs = (count - 1) // 2
    donor, taker = sizes[1:1 + 2 * pairs:2], sizes[2:2 + 2 * pairs:2]
    room = jnp.minimum(donor - 1, most - taker)
    passed = jax.random.randint(jax.random.fold_in(key, 1), (pairs,), 0, 1 << 20) % (room + 1)
    sizes = sizes.at[1:1 + 2 * pairs:2].set(donor - passed).at[2:2 + 2 * pairs:2].set(taker + passed)
    return sizes[jax.random.permutation(jax.random.fold_in(key, 2), count)]


def normal_values(rng, extent, width, limit, cuts=(), held_as=jnp.bfloat16):
    gain = shard_levels(rng, extent, cuts, -0.22, 0.18) if cuts else 1.0
    values = jax.random.normal(rng, extent, jnp.float32) * width * gain
    return jnp.minimum(jnp.maximum(values, -limit), limit).astype(held_as)


def setup_inputs(seed: int = 0) -> dict:
    arg_keys = jax.random.split(jax.random.key(seed), 13)
    tokens = normal_values(arg_keys[0], (TOKENS, D), 1.0, 6.0, ((0, 32),))
    lengths = jax.vmap(lambda own: uneven(own, SEQS_DEV, TOK_DEV, SEQ_MOST, 2))(jax.random.split(arg_keys[1], DEVICES)).reshape((DEVICES, SEQS_DEV)).astype(jnp.int32)
    routes = picks_of(arg_keys[2], TOKENS, EXPERTS, 1, 8192)
    buckets = place_ends(jax.random.randint(arg_keys[3], (2 * TOK_DEV - 1,), 0, BUCKETS), jax.random.fold_in(arg_keys[3], 1), 0, BUCKETS - 1).astype(jnp.int32)
    bias_table = normal_values(arg_keys[4], (BUCKETS, HEADS), 1.0, 5.0, (), jnp.float32)
    projection = normal_values(arg_keys[5], (LAYERS, D, 3 * D), D ** -0.5, 0.21875, ((1, 16),))
    collector = normal_values(arg_keys[6], (LAYERS, D, D), (D // 16) ** -0.5, 0.875, ((1, 16),))
    router = normal_values(arg_keys[7], (LAYERS, D, EXPERTS), (2 * D) ** -0.5, 0.15625, ((1, 16),))
    scales = jnp.clip(1.0 + 0.18 * jax.random.normal(arg_keys[8], (LAYERS, D, 2), jnp.float32), 0.099609375, 1.8984375).astype(jnp.bfloat16)
    upward = normal_values(arg_keys[9], (LAYERS, EXPERTS, D, FF), D ** -0.5, 0.21875, ((1, 2), (3, 4)))
    downward = normal_values(arg_keys[10], (LAYERS, EXPERTS, FF, D), (FF // 64) ** -0.5, 0.875, ((1, 2), (2, 4)))
    cotangent = normal_values(arg_keys[11], (TOKENS, D), 1.0, 6.0, ((0, 32),))
    return dict(tokens=tokens, lengths=lengths, routes=routes, buckets=buckets, bias_table=bias_table, projection=projection, collector=collector, router=router, scales=scales, upward=upward, downward=downward, cotangent=cotangent)


EPSILON = 1e-06
NEG_FILL = -1e+30
HIGHEST = lax.Precision.HIGHEST

@jax.custom_vjp
def low(v):
    return lax.optimization_barrier(v.astype(jnp.bfloat16)).astype(jnp.float32)

@jax.custom_vjp
def low_back(v):
    return v

def low_keep(v):
    return (low(v), None)

def low_pass(kept, grad):
    return (grad,)

def back_keep(v):
    return (v, None)

def back_low(kept, grad):
    return (low(grad),)
low.defvjp(low_keep, low_pass)
low_back.defvjp(back_keep, back_low)

def rounded(inputs):
    return low(low_back(inputs))

def normalize(inputs, gain_vector):
    scale_rows = lax.rsqrt(lax.optimization_barrier(jnp.mean(inputs * inputs, axis=-1, keepdims=True)) + EPSILON)
    return inputs * scale_rows * gain_vector

def attend(residual, same_segment, proj_layer, collect_layer, gain_one, bias_heads):
    tokens_dev = residual.shape[0]
    hidden_one = low(normalize(residual, gain_one))
    packed = rounded(jnp.dot(hidden_one, proj_layer, precision=HIGHEST))
    queries = packed[:, :D].reshape(tokens_dev, HEADS, HEAD_DIM)
    key_heads = packed[:, D:2 * D].reshape(tokens_dev, HEADS, HEAD_DIM)
    value_heads = packed[:, 2 * D:].reshape(tokens_dev, HEADS, HEAD_DIM)
    scores = jnp.einsum('thd,shd->hts', queries, key_heads, precision=HIGHEST) * HEAD_DIM ** (-0.5) + bias_heads
    scores = low_back(scores)
    scores = jnp.where(same_segment[None], scores, NEG_FILL)
    row_peak = lax.optimization_barrier(jnp.max(scores, axis=-1, keepdims=True))
    weights = jnp.exp(scores - row_peak)
    attention = weights / lax.optimization_barrier(jnp.sum(weights, axis=-1, keepdims=True))
    mixed_heads = jnp.einsum('hts,shd->thd', low(attention), value_heads, precision=HIGHEST)
    mixed_heads = rounded(mixed_heads.reshape(tokens_dev, D))
    return residual + low_back(jnp.dot(mixed_heads, collect_layer, precision=HIGHEST))

def expert_apply(triple):
    rows_all, up_layer, down_layer = triple
    hidden_pre = low_back(jnp.dot(rows_all, up_layer, precision=HIGHEST))
    hidden_act = low(jax.nn.gelu(hidden_pre))
    return rounded(jnp.dot(hidden_act, down_layer, precision=HIGHEST))

def reference(tokens, lengths, routes, buckets, bias_table, projection, collector, router, scales, upward, downward, cotangent):
    devices_all = lengths.shape[0]
    places = jnp.arange(TOK_DEV, dtype=jnp.int32)
    bounds = jnp.cumsum(lengths, axis=1)
    segment = lax.optimization_barrier(jnp.sum((places[None, :, None] >= bounds[:, None, :]).astype(jnp.int32), axis=2))
    same_all = segment[:, :, None] == segment[:, None, :]
    offsets = (places[None, :] - places[:, None] + TOK_DEV - 1).astype(jnp.int32)
    pair_bucket = buckets[offsets]
    chosen = routes[:, 0].reshape(devices_all, TOK_DEV)
    route_hot = (chosen[:, :, None] == jnp.arange(EXPERTS, dtype=jnp.int32)[None, None, :]).astype(jnp.int32)
    position = lax.optimization_barrier(jnp.sum(jnp.cumsum(route_hot, axis=1) * route_hot, axis=2)) - 1
    retained = position < CAP
    device_ids = jnp.arange(devices_all, dtype=jnp.int32)[:, None]
    dump_index = EXPERTS * devices_all * CAP
    slot_index = jnp.where(retained, (chosen * devices_all + device_ids) * CAP + position, dump_index).reshape(-1).astype(jnp.int32)
    kept_float = retained.reshape(-1).astype(jnp.float32)
    route_float = route_hot.reshape(-1, EXPERTS).astype(jnp.float32)

    def forward(residual, table_values, proj_all, collect_all, router_all, scales_all, up_all, down_all):
        bias_heads = jnp.transpose(table_values[pair_bucket], (2, 0, 1))
        for layer in range(LAYERS):
            gain_one = scales_all[layer, :, 0]
            gain_two = scales_all[layer, :, 1]
            proj_layer = proj_all[layer]
            collect_layer = collect_all[layer]
            blocks = residual.reshape(devices_all, TOK_DEV, D)
            middle = lax.map(jax.checkpoint(lambda pair: attend(pair[0], pair[1], proj_layer, collect_layer, gain_one, bias_heads)), (blocks, same_all))
            middle = middle.reshape(-1, D)
            normed_two = normalize(middle, gain_two)
            logits = jnp.dot(normed_two, router_all[layer], precision=HIGHEST)
            gate_probs = jax.nn.softmax(logits, axis=-1)
            gate_value = lax.optimization_barrier(jnp.sum(gate_probs * route_float, axis=1)) * kept_float
            sent = rounded(normed_two)
            buffer = jnp.zeros((dump_index + 1, D), jnp.float32).at[slot_index].set(sent)
            expert_rows = buffer[:-1].reshape(EXPERTS, devices_all * CAP, D)
            returned = lax.map(jax.checkpoint(expert_apply), (expert_rows, up_all[layer], down_all[layer]))
            flat_rows = jnp.concatenate([returned.reshape(-1, D), jnp.zeros((1, D), jnp.float32)], axis=0)
            residual = middle + gate_value[:, None] * flat_rows[slot_index]
        return residual
    floats = (tokens.astype(jnp.float32), bias_table.astype(jnp.float32), projection.astype(jnp.float32), collector.astype(jnp.float32), router.astype(jnp.float32), scales.astype(jnp.float32), upward.astype(jnp.float32), downward.astype(jnp.float32))
    result, pullback = jax.vjp(forward, *floats)
    grads = pullback(cotangent.astype(jnp.float32))
    return (result.astype(jnp.bfloat16), grads[0], grads[2], grads[3], grads[4], grads[5], grads[6], grads[7], grads[1])
```

```python
import jax
import jax.numpy as jnp
from jax import lax
from jax.sharding import PartitionSpec as P

HEADS = 12
HEAD_DIM = 64


EPSILON = 1e-06
NEG_FILL = -1e30
HIGHEST = lax.Precision.HIGHEST


def rms_forward(inputs, gain_vector):
    scale_rows = lax.rsqrt(jnp.mean(inputs * inputs, axis=-1, keepdims=True) + EPSILON)
    normed = inputs * scale_rows
    return (normed * gain_vector, normed, scale_rows)


def rms_backward(grad_output, gain_vector, normed, scale_rows):
    grad_normed = grad_output * gain_vector
    grad_gain = jnp.sum(grad_output * normed, axis=0)
    grad_inputs = scale_rows * (
        grad_normed - normed * jnp.mean(grad_normed * normed, axis=-1, keepdims=True)
    )
    return (grad_inputs, grad_gain)


def send_rows(buffer):
    return lax.all_to_all(buffer, "expert", split_axis=0, concat_axis=0, tiled=True)


def return_rows(buffer):
    return lax.all_to_all(buffer, "expert", split_axis=0, concat_axis=0, tiled=True)


def spread_rows(arrived):
    return lax.all_gather(arrived, "shard", axis=0, tiled=True)


def sum_hidden(partial_value):
    return lax.psum_scatter(
        partial_value.astype(jnp.bfloat16), "shard", scatter_dimension=0, tiled=True
    ).astype(jnp.float32)


def pair_moves(axis_size, stride, count, shift):
    moves = []
    for place in range(axis_size):
        part = (place // stride) % count
        moves.append((place, place + ((part + shift) % count - part) * stride))
    return moves


def scatter_sum(parts, axis, stride, count):
    axis_size = lax.axis_size(axis)
    mine = (lax.axis_index(axis) // stride) % count
    total = lax.dynamic_index_in_dim(parts, mine, 0, keepdims=False).astype(jnp.float32)
    for shift in range(1, count):
        leaving = lax.dynamic_index_in_dim(parts, (mine + shift) % count, 0, keepdims=False)
        total = total + lax.ppermute(
            leaving, axis, pair_moves(axis_size, stride, count, shift)
        ).astype(jnp.float32)
    return total.astype(jnp.bfloat16)


def dp_levels():
    size = lax.axis_size("dp")
    low = 2 if size % 2 == 0 else 1
    return size // low, low


def reduce_experts(grad_up, grad_down_t):
    high, low = dp_levels()
    rows, columns = grad_up.shape
    both = jnp.stack([grad_up.astype(jnp.bfloat16), grad_down_t.astype(jnp.bfloat16)])
    both = both.reshape(2, high, low, rows // (high * low), columns)
    part = scatter_sum(jnp.moveaxis(both, 2, 0), "dp", 1, low)
    part = scatter_sum(jnp.moveaxis(part, 1, 0), "dp", low, high)
    return part[0].astype(jnp.float32), part[1].astype(jnp.float32)


def reduce_mixer(grads):
    high, low = dp_levels()
    owners, experts = lax.axis_size("shard"), lax.axis_size("expert")
    widths = [grad.shape[1] for grad in grads]
    unit = 128 * experts
    spare = -sum(widths) % unit
    rows = grads[0].shape[0]
    packed = jnp.concatenate(
        [grad.astype(jnp.bfloat16) for grad in grads] + [jnp.zeros((rows, spare), jnp.bfloat16)],
        axis=1,
    )
    block = rows // (owners * high * low)
    chunk = packed.shape[1] // experts
    packed = packed.reshape(owners, high, low, block, packed.shape[1])
    part = scatter_sum(jnp.moveaxis(packed, 2, 0), "dp", 1, low)
    part = jnp.stack([part[..., at * chunk : (at + 1) * chunk] for at in range(experts)])
    part = scatter_sum(part, "expert", 1, experts)
    part = scatter_sum(jnp.moveaxis(part, 1, 0), "dp", low, high)
    part = scatter_sum(part, "shard", 1, owners)
    if experts == 2:
        other = lax.ppermute(part, "expert", pair_moves(2, 1, 2, 1))
        first = lax.axis_index("expert") == 0
        whole = jnp.concatenate(
            [jnp.where(first, part, other), jnp.where(first, other, part)], axis=1
        )
    else:
        whole = lax.all_gather(part, "expert", axis=1, tiled=True)
    whole = whole.astype(jnp.float32)
    shares, start = [], 0
    for width in widths:
        shares.append(whole[:, start : start + width])
        start += width
    return shares


def fetch_mixer(projection, collector, router, scales, layer):
    pieces = (projection[layer], collector[layer], router[layer], scales[layer])
    widths = [piece.shape[1] for piece in pieces]
    spare = -sum(widths) % 128
    packed = jnp.concatenate(
        pieces + (jnp.zeros((pieces[0].shape[0], spare), jnp.bfloat16),), axis=1
    )
    whole = lax.all_gather(packed, ("shard", "dp"), axis=0, tiled=True)
    fetched, start = [], 0
    for width in widths:
        fetched.append(whole[:, start : start + width])
        start += width
    return tuple(fetched)


def score_heads(queries, key_heads, bias_heads, same_segment):
    scores = (
        jnp.einsum("thd,shd->hts", queries, key_heads, preferred_element_type=jnp.float32)
        * HEAD_DIM ** (-0.5)
        + bias_heads
    )
    return jnp.where(same_segment[None], scores, NEG_FILL)


def offsets_to_pairs(offset_rows, tokens_dev):
    heads_all = offset_rows.shape[0]
    padded = jnp.pad(offset_rows, ((0, 0), (0, 1)))
    tiled = jnp.tile(padded, (1, tokens_dev))
    window = tiled[:, tokens_dev - 1 : tokens_dev - 1 + tokens_dev * (2 * tokens_dev - 1)]
    return window.reshape(heads_all, tokens_dev, 2 * tokens_dev - 1)[:, :, :tokens_dev]


def pairs_to_offsets(pair_values, tokens_dev):
    heads_all = pair_values.shape[0]
    widened = jnp.pad(pair_values, ((0, 0), (0, 0), (0, tokens_dev - 1)))
    flat = widened.reshape(heads_all, tokens_dev * (2 * tokens_dev - 1))
    flat = jnp.pad(flat, ((0, 0), (tokens_dev - 1, 1)))
    folded = jnp.sum(flat.reshape(heads_all, tokens_dev, 2 * tokens_dev), axis=1)
    return folded[:, : 2 * tokens_dev - 1]


def body(
    tokens,
    lengths,
    routes,
    buckets,
    bias_table,
    projection,
    collector,
    router,
    scales,
    upward,
    downward,
    cotangent,
):
    tokens_dev, model_width = tokens.shape
    layers = projection.shape[0]
    experts = router.shape[2]
    capacity = 5 * tokens_dev // (4 * experts)
    buckets_all = bias_table.shape[0]
    head_scale = HEAD_DIM ** (-0.5)
    places = jnp.arange(tokens_dev, dtype=jnp.int32)
    bounds = jnp.cumsum(lengths[0])
    segment = jnp.sum((places[:, None] >= bounds[None, :]).astype(jnp.int32), axis=1)
    same_segment = segment[:, None] == segment[None, :]
    offset_hot = (buckets[:, None] == jnp.arange(buckets_all, dtype=jnp.int32)[None, :]).astype(
        jnp.float32
    )
    offset_bias = jnp.dot(offset_hot, bias_table, precision=HIGHEST).T
    bias_heads = offsets_to_pairs(offset_bias, tokens_dev)
    chosen = routes[:, 0]
    route_hot = (chosen[:, None] == jnp.arange(experts, dtype=jnp.int32)[None, :]).astype(jnp.int32)
    position = jnp.sum(jnp.cumsum(route_hot, axis=0) * route_hot, axis=1) - 1
    retained = (position < capacity).astype(jnp.float32)
    slot_index = chosen * capacity + position
    slot_hot = (
        slot_index[:, None] == jnp.arange(experts * capacity, dtype=jnp.int32)[None, :]
    ).astype(jnp.float32)
    slot_hot = (slot_hot * retained[:, None]).astype(jnp.bfloat16)
    slot_back = slot_hot.T
    route_float = route_hot.astype(jnp.float32)
    residual = tokens.astype(jnp.float32)
    stored = []
    gathered = [
        fetch_mixer(projection, collector, router, scales, layer) for layer in range(layers)
    ]
    for layer in range(layers):
        fetched = gathered[layer]
        proj_full, collect_full, router_full, scales_full = fetched
        gain_one = scales_full[:, 0].astype(jnp.float32)
        gain_two = scales_full[:, 1].astype(jnp.float32)
        normed_one, base_one, scale_one = rms_forward(residual, gain_one)
        hidden_one = normed_one.astype(jnp.bfloat16)
        packed = jnp.dot(hidden_one, proj_full, preferred_element_type=jnp.float32).astype(
            jnp.bfloat16
        )
        queries = packed[:, :model_width].reshape(tokens_dev, HEADS, HEAD_DIM)
        key_heads = packed[:, model_width : 2 * model_width].reshape(tokens_dev, HEADS, HEAD_DIM)
        value_heads = packed[:, 2 * model_width :].reshape(tokens_dev, HEADS, HEAD_DIM)
        scores = score_heads(queries, key_heads, bias_heads, same_segment)
        row_peak = jnp.max(scores, axis=-1, keepdims=True)
        log_total = row_peak + jnp.log(jnp.sum(jnp.exp(scores - row_peak), axis=-1, keepdims=True))
        attention = jnp.exp(scores - log_total)
        mixed_heads = jnp.einsum(
            "hts,shd->thd",
            attention.astype(jnp.bfloat16),
            value_heads,
            preferred_element_type=jnp.float32,
        )
        mixed_heads = mixed_heads.reshape(tokens_dev, model_width).astype(jnp.bfloat16)
        middle = residual + jnp.dot(mixed_heads, collect_full, preferred_element_type=jnp.float32)
        normed_two, base_two, scale_two = rms_forward(middle, gain_two)
        router_float = router_full.astype(jnp.float32)
        logits = jnp.dot(normed_two, router_float, precision=HIGHEST)
        gate_probs = jax.nn.softmax(logits, axis=-1)
        gate_value = jnp.sum(gate_probs * route_float, axis=1) * retained
        sent = normed_two.astype(jnp.bfloat16)
        buffer = jnp.dot(slot_back, sent, preferred_element_type=jnp.float32).astype(jnp.bfloat16)
        arrived = send_rows(buffer.reshape(experts, capacity, model_width)).reshape(
            experts * capacity, model_width
        )
        rows_all = spread_rows(arrived)
        hidden_pre = jnp.dot(rows_all, upward[layer, 0], preferred_element_type=jnp.float32)
        hidden_act = jax.nn.gelu(hidden_pre).astype(jnp.bfloat16)
        partial_value = jnp.dot(hidden_act, downward[layer, 0], preferred_element_type=jnp.float32)
        expert_sum = (
            sum_hidden(partial_value).astype(jnp.bfloat16).reshape(experts, capacity, model_width)
        )
        returned = return_rows(expert_sum).reshape(experts * capacity, model_width)
        expert_tokens = jnp.dot(slot_hot, returned, preferred_element_type=jnp.float32)
        residual = middle + gate_value[:, None] * expert_tokens
        stored.append(
            dict(
                fetched=fetched,
                base_one=base_one,
                scale_one=scale_one,
                hidden_one=hidden_one,
                queries=queries,
                key_heads=key_heads,
                value_heads=value_heads,
                log_total=log_total,
                mixed_heads=mixed_heads,
                base_two=base_two,
                scale_two=scale_two,
                normed_two=normed_two,
                gate_probs=gate_probs,
                gate_value=gate_value,
                rows_all=rows_all,
                hidden_pre=hidden_pre,
                hidden_act=hidden_act,
                expert_tokens=expert_tokens,
            )
        )
    grad_residual = cotangent.astype(jnp.float32)
    offset_total = jnp.zeros((HEADS, 2 * tokens_dev - 1), jnp.float32)
    proj_grads, collect_grads, router_grads, scale_grads, up_grads, down_grads = (
        [],
        [],
        [],
        [],
        [],
        [],
    )
    for layer in reversed(range(layers)):
        saved_layer = stored[layer]
        proj_full, collect_full, router_full, scales_full = saved_layer["fetched"]
        gain_one = scales_full[:, 0].astype(jnp.float32)
        gain_two = scales_full[:, 1].astype(jnp.float32)
        router_float = router_full.astype(jnp.float32)
        gate_value = saved_layer["gate_value"]
        gate_probs = saved_layer["gate_probs"]
        grad_gate = jnp.sum(grad_residual * saved_layer["expert_tokens"], axis=1)
        grad_tokens_out = (gate_value[:, None] * grad_residual).astype(jnp.bfloat16)
        grad_buffer = jnp.dot(
            slot_back, grad_tokens_out, preferred_element_type=jnp.float32
        ).astype(jnp.bfloat16)
        grad_arrived = send_rows(grad_buffer.reshape(experts, capacity, model_width)).reshape(
            experts * capacity, model_width
        )
        grad_spread = spread_rows(grad_arrived)
        grad_act = jnp.dot(grad_spread, downward[layer, 0].T, preferred_element_type=jnp.float32)
        gelu_value, gelu_pull = jax.vjp(jax.nn.gelu, saved_layer["hidden_pre"])
        grad_pre = gelu_pull(grad_act)[0].astype(jnp.bfloat16)
        grad_down_t = jnp.dot(
            grad_spread.T, saved_layer["hidden_act"], preferred_element_type=jnp.float32
        )
        grad_up = jnp.dot(saved_layer["rows_all"].T, grad_pre, preferred_element_type=jnp.float32)
        grad_sent_part = jnp.dot(grad_pre, upward[layer, 0].T, preferred_element_type=jnp.float32)
        grad_sent = (
            sum_hidden(grad_sent_part).astype(jnp.bfloat16).reshape(experts, capacity, model_width)
        )
        grad_back = return_rows(grad_sent).reshape(experts * capacity, model_width)
        grad_normed_two = jnp.dot(slot_hot, grad_back, preferred_element_type=jnp.float32)
        grad_gprobs = (grad_gate * retained)[:, None] * route_float
        grad_logits = gate_probs * (
            grad_gprobs - jnp.sum(grad_gprobs * gate_probs, axis=1, keepdims=True)
        )
        grad_router = jnp.dot(saved_layer["normed_two"].T, grad_logits, precision=HIGHEST)
        grad_normed_two = grad_normed_two + jnp.dot(grad_logits, router_float.T, precision=HIGHEST)
        grad_mid_norm, grad_gain_two = rms_backward(
            grad_normed_two, gain_two, saved_layer["base_two"], saved_layer["scale_two"]
        )
        grad_middle = grad_residual + grad_mid_norm
        grad_branch = grad_middle.astype(jnp.bfloat16)
        grad_collect = jnp.dot(
            saved_layer["mixed_heads"].T, grad_branch, preferred_element_type=jnp.float32
        )
        grad_mixed = jnp.dot(
            grad_branch, collect_full.T, preferred_element_type=jnp.float32
        ).astype(jnp.bfloat16)
        grad_mixed = grad_mixed.reshape(tokens_dev, HEADS, HEAD_DIM)
        queries = saved_layer["queries"]
        key_heads = saved_layer["key_heads"]
        value_heads = saved_layer["value_heads"]
        scores = score_heads(queries, key_heads, bias_heads, same_segment)
        attention = jnp.exp(scores - saved_layer["log_total"])
        grad_values = jnp.einsum(
            "hts,thd->shd",
            attention.astype(jnp.bfloat16),
            grad_mixed,
            preferred_element_type=jnp.float32,
        )
        grad_attention = jnp.einsum(
            "thd,shd->hts", grad_mixed, value_heads, preferred_element_type=jnp.float32
        )
        grad_scores = attention * (
            grad_attention - jnp.sum(grad_attention * attention, axis=-1, keepdims=True)
        )
        grad_scores_low = grad_scores.astype(jnp.bfloat16)
        grad_queries = (
            jnp.einsum(
                "hts,shd->thd", grad_scores_low, key_heads, preferred_element_type=jnp.float32
            )
            * head_scale
        )
        grad_keys = (
            jnp.einsum("hts,thd->shd", grad_scores_low, queries, preferred_element_type=jnp.float32)
            * head_scale
        )
        offset_total = offset_total + pairs_to_offsets(
            grad_scores_low.astype(jnp.float32), tokens_dev
        )
        grad_packed = jnp.concatenate(
            [
                grad_queries.reshape(tokens_dev, model_width),
                grad_keys.reshape(tokens_dev, model_width),
                grad_values.reshape(tokens_dev, model_width),
            ],
            axis=1,
        ).astype(jnp.bfloat16)
        grad_proj = jnp.dot(
            saved_layer["hidden_one"].T, grad_packed, preferred_element_type=jnp.float32
        )
        grad_hidden_one = jnp.dot(grad_packed, proj_full.T, preferred_element_type=jnp.float32)
        grad_in_norm, grad_gain_one = rms_backward(
            grad_hidden_one, gain_one, saved_layer["base_one"], saved_layer["scale_one"]
        )
        grad_residual = grad_middle + grad_in_norm
        grad_scales = jnp.stack([grad_gain_one, grad_gain_two], axis=1)
        expert_shares = reduce_experts(grad_up, grad_down_t)
        shares = reduce_mixer([grad_proj, grad_collect, grad_router, grad_scales])
        proj_grads.insert(0, shares[0])
        collect_grads.insert(0, shares[1])
        router_grads.insert(0, shares[2])
        scale_grads.insert(0, shares[3])
        up_grads.insert(0, expert_shares[0][None])
        down_grads.insert(0, expert_shares[1].T[None])
    table_total = jnp.dot(offset_total, offset_hot, precision=HIGHEST).T
    table_sum = lax.psum(table_total, ("expert", "shard", "dp"))
    return (
        residual.astype(jnp.bfloat16),
        grad_residual,
        jnp.stack(proj_grads),
        jnp.stack(collect_grads),
        jnp.stack(router_grads),
        jnp.stack(scale_grads),
        jnp.stack(up_grads),
        jnp.stack(down_grads),
        table_sum,
    )


def solution(mesh):
    in_specs = (
        P(("expert", "shard", "dp"), None),
        P(("expert", "shard", "dp"), None),
        P(("expert", "shard", "dp"), None),
        P(),
        P(),
        P(None, ("shard", "dp"), None),
        P(None, ("shard", "dp"), None),
        P(None, ("shard", "dp"), None),
        P(None, ("shard", "dp"), None),
        P(None, "expert", None, "shard"),
        P(None, "expert", "shard", None),
        P(("expert", "shard", "dp"), None),
    )
    out_specs = (
        P(("expert", "shard", "dp"), None),
        P(("expert", "shard", "dp"), None),
        P(None, ("shard", "dp"), None),
        P(None, ("shard", "dp"), None),
        P(None, ("shard", "dp"), None),
        P(None, ("shard", "dp"), None),
        P(None, "expert", "dp", "shard"),
        P(None, "expert", "shard", "dp"),
        P(),
    )
    return jax.shard_map(body, mesh=mesh, in_specs=in_specs, out_specs=out_specs, check_vma=False)
```

```python
import jax
import jax.numpy as jnp
from jax import lax
from jax.sharding import PartitionSpec as P

HEADS = 12
HEAD_DIM = 64


EPSILON = 1e-06
NEG_FILL = -1e30
HIGHEST = lax.Precision.HIGHEST


def rms_forward(inputs, gain_vector):
    scale_rows = lax.rsqrt(jnp.mean(inputs * inputs, axis=-1, keepdims=True) + EPSILON)
    normed = inputs * scale_rows
    return (normed * gain_vector, normed, scale_rows)


def rms_backward(grad_output, gain_vector, normed, scale_rows):
    grad_normed = grad_output * gain_vector
    grad_gain = jnp.sum(grad_output * normed, axis=0)
    grad_inputs = scale_rows * (
        grad_normed - normed * jnp.mean(grad_normed * normed, axis=-1, keepdims=True)
    )
    return (grad_inputs, grad_gain)


def pair_moves(axis_size, stride, count, shift):
    moves = []
    for place in range(axis_size):
        part = (place // stride) % count
        moves.append((place, place + ((part + shift) % count - part) * stride))
    return moves


def send_rows(parts):
    experts, owners = lax.axis_size("expert"), lax.axis_size("shard")
    mine = lax.axis_index("expert")
    blocks = []
    for away in range(experts):
        piece = lax.dynamic_index_in_dim(parts, (mine + away) % experts, 0, keepdims=False)
        if away:
            piece = lax.ppermute(piece, "expert", pair_moves(experts, 1, experts, away))
        blocks.append(piece)
        for shift in range(1, owners):
            blocks.append(lax.ppermute(piece, "shard", pair_moves(owners, 1, owners, shift)))
    return jnp.concatenate(blocks)


def return_rows(partial_value):
    experts, owners = lax.axis_size("expert"), lax.axis_size("shard")
    mine = lax.axis_index("expert")
    parts = partial_value.astype(jnp.bfloat16)
    parts = parts.reshape(experts, owners, -1, partial_value.shape[1])
    result = jnp.zeros((experts,) + parts.shape[2:], jnp.bfloat16)
    for away in reversed(range(experts)):
        total = parts[away, 0].astype(jnp.float32)
        for shift in range(1, owners):
            total = total + lax.ppermute(
                parts[away, shift], "shard", pair_moves(owners, 1, owners, owners - shift)
            ).astype(jnp.float32)
        total = total.astype(jnp.bfloat16)
        if away:
            total = lax.ppermute(total, "expert", pair_moves(experts, 1, experts, experts - away))
        result = lax.dynamic_update_index_in_dim(result, total, (mine + away) % experts, 0)
    return result.reshape(-1, partial_value.shape[1])


def scatter_sum(parts, axis, stride, count):
    axis_size = lax.axis_size(axis)
    mine = (lax.axis_index(axis) // stride) % count
    total = lax.dynamic_index_in_dim(parts, mine, 0, keepdims=False).astype(jnp.float32)
    for shift in range(1, count):
        leaving = lax.dynamic_index_in_dim(parts, (mine + shift) % count, 0, keepdims=False)
        total = total + lax.ppermute(
            leaving, axis, pair_moves(axis_size, stride, count, shift)
        ).astype(jnp.float32)
    return total.astype(jnp.bfloat16)


def dp_levels():
    size = lax.axis_size("dp")
    low = 2 if size % 2 == 0 else 1
    return size // low, low


def reduce_experts(grad_up, grad_down_t):
    high, low = dp_levels()
    rows, columns = grad_up.shape
    both = jnp.stack([grad_up.astype(jnp.bfloat16), grad_down_t.astype(jnp.bfloat16)])
    both = both.reshape(2, high, low, rows // (high * low), columns)
    part = scatter_sum(jnp.moveaxis(both, 2, 0), "dp", 1, low)
    part = scatter_sum(jnp.moveaxis(part, 1, 0), "dp", low, high)
    return part[0].astype(jnp.float32), part[1].astype(jnp.float32)


def reduce_rows(grad):
    high, low = dp_levels()
    owners, experts = lax.axis_size("shard"), lax.axis_size("expert")
    block = grad.shape[0] // (owners * high * low)
    chunk = grad.shape[1] // experts
    packed = grad.astype(jnp.bfloat16).reshape(owners, high, low, block, grad.shape[1])
    part = scatter_sum(jnp.moveaxis(packed, 2, 0), "dp", 1, low)
    part = jnp.stack([part[..., at * chunk : (at + 1) * chunk] for at in range(experts)])
    part = scatter_sum(part, "expert", 1, experts)
    part = scatter_sum(jnp.moveaxis(part, 1, 0), "dp", low, high)
    part = scatter_sum(part, "shard", 1, owners)
    if experts == 2:
        other = lax.ppermute(part, "expert", pair_moves(2, 1, 2, 1))
        first = lax.axis_index("expert") == 0
        whole = jnp.concatenate(
            [jnp.where(first, part, other), jnp.where(first, other, part)], axis=1
        )
    else:
        whole = lax.all_gather(part, "expert", axis=1, tiled=True)
    return whole.astype(jnp.float32)


def sum_everywhere(value):
    for axis in ("dp", "expert", "shard"):
        size = lax.axis_size(axis)
        if size & (size - 1):
            value = lax.psum(value, axis)
            continue
        stride = 1
        while stride < size:
            value = value + lax.ppermute(value, axis, pair_moves(size, stride, 2, 1))
            stride *= 2
    return value


def gather_level(block, axis, stride, count):
    axis_size = lax.axis_size(axis)
    mine = (lax.axis_index(axis) // stride) % count
    whole = jnp.zeros((count,) + block.shape, block.dtype)
    whole = lax.dynamic_update_index_in_dim(whole, block, mine, 0)
    for shift in range(1, count):
        piece = lax.ppermute(block, axis, pair_moves(axis_size, stride, count, shift))
        whole = lax.dynamic_update_index_in_dim(whole, piece, (mine - shift) % count, 0)
    return whole


def gather_rows(block):
    high, low = dp_levels()
    whole = gather_level(block, "shard", 1, lax.axis_size("shard"))
    whole = gather_level(whole, "dp", low, high)
    whole = gather_level(whole, "dp", 1, low)
    whole = jnp.moveaxis(whole, (0, 1, 2), (2, 1, 0))
    return whole.reshape(-1, block.shape[1])


def pack_mixer(projection, collector, router, scales, layer):
    pieces = (collector[layer], router[layer], scales[layer])
    spare = -sum(piece.shape[1] for piece in pieces) % 128
    zeros = jnp.zeros((pieces[0].shape[0], spare), jnp.bfloat16)
    return projection[layer], jnp.concatenate(pieces + (zeros,), axis=1)


def cut_mixer(proj_full, packed, experts):
    width = proj_full.shape[0]
    return (
        proj_full,
        packed[:, :width],
        packed[:, width : width + experts],
        packed[:, width + experts : width + experts + 2],
    )


def fetch_first(projection, collector, router, scales):
    proj, packed = pack_mixer(projection, collector, router, scales, 0)
    thirds = jnp.split(proj, 3, axis=1)
    packed_full = gather_rows(packed)
    proj_full = jnp.concatenate([gather_rows(third) for third in thirds], axis=1)
    return cut_mixer(proj_full, packed_full, router.shape[2])


def fetch_later(projection, collector, router, scales, layer, after):
    proj, packed = pack_mixer(projection, collector, router, scales, layer)
    both = jnp.concatenate([proj, packed], axis=1)
    both, after = lax.optimization_barrier((both, after))
    whole = lax.all_gather(both, ("shard", "dp"), axis=0, tiled=True)
    return cut_mixer(whole[:, : proj.shape[1]], whole[:, proj.shape[1] :], router.shape[2]), after


def score_heads(queries, key_heads, bias_heads, same_segment):
    scores = (
        jnp.einsum("thd,shd->hts", queries, key_heads, preferred_element_type=jnp.float32)
        * HEAD_DIM ** (-0.5)
        + bias_heads
    )
    return jnp.where(same_segment[None], scores, NEG_FILL)


def offsets_to_pairs(offset_rows, tokens_dev):
    heads_all = offset_rows.shape[0]
    padded = jnp.pad(offset_rows, ((0, 0), (0, 1)))
    tiled = jnp.tile(padded, (1, tokens_dev))
    window = tiled[:, tokens_dev - 1 : tokens_dev - 1 + tokens_dev * (2 * tokens_dev - 1)]
    return window.reshape(heads_all, tokens_dev, 2 * tokens_dev - 1)[:, :, :tokens_dev]


def pairs_to_offsets(pair_values, tokens_dev):
    heads_all = pair_values.shape[0]
    widened = jnp.pad(pair_values, ((0, 0), (0, 0), (0, tokens_dev - 1)))
    flat = widened.reshape(heads_all, tokens_dev * (2 * tokens_dev - 1))
    flat = jnp.pad(flat, ((0, 0), (tokens_dev - 1, 1)))
    folded = jnp.sum(flat.reshape(heads_all, tokens_dev, 2 * tokens_dev), axis=1)
    return folded[:, : 2 * tokens_dev - 1]


def body(
    tokens,
    lengths,
    routes,
    buckets,
    bias_table,
    projection,
    collector,
    router,
    scales,
    upward,
    downward,
    cotangent,
):
    tokens_dev, model_width = tokens.shape
    layers = projection.shape[0]
    experts = router.shape[2]
    capacity = 5 * tokens_dev // (4 * experts)
    buckets_all = bias_table.shape[0]
    head_scale = HEAD_DIM ** (-0.5)
    places = jnp.arange(tokens_dev, dtype=jnp.int32)
    bounds = jnp.cumsum(lengths[0])
    segment = jnp.sum((places[:, None] >= bounds[None, :]).astype(jnp.int32), axis=1)
    same_segment = segment[:, None] == segment[None, :]
    offset_hot = (buckets[:, None] == jnp.arange(buckets_all, dtype=jnp.int32)[None, :]).astype(
        jnp.float32
    )
    offset_bias = jnp.dot(offset_hot, bias_table, precision=HIGHEST).T
    bias_heads = offsets_to_pairs(offset_bias, tokens_dev)
    chosen = routes[:, 0]
    route_hot = (chosen[:, None] == jnp.arange(experts, dtype=jnp.int32)[None, :]).astype(jnp.int32)
    position = jnp.sum(jnp.cumsum(route_hot, axis=0) * route_hot, axis=1) - 1
    retained = (position < capacity).astype(jnp.float32)
    slot_index = chosen * capacity + position
    slot_hot = (
        slot_index[:, None] == jnp.arange(experts * capacity, dtype=jnp.int32)[None, :]
    ).astype(jnp.float32)
    slot_hot = (slot_hot * retained[:, None]).astype(jnp.bfloat16)
    slot_back = slot_hot.T
    route_float = route_hot.astype(jnp.float32)
    residual = tokens.astype(jnp.float32)
    stored = []
    gathered = {0: fetch_first(projection, collector, router, scales)}
    for layer in range(layers):
        fetched = gathered[layer]
        proj_full, collect_full, router_full, scales_full = fetched
        gain_one = scales_full[:, 0].astype(jnp.float32)
        gain_two = scales_full[:, 1].astype(jnp.float32)
        normed_one, base_one, scale_one = rms_forward(residual, gain_one)
        hidden_one = normed_one.astype(jnp.bfloat16)
        packed = jnp.dot(hidden_one, proj_full, preferred_element_type=jnp.float32).astype(
            jnp.bfloat16
        )
        if layer + 1 < layers:
            gathered[layer + 1], packed = fetch_later(
                projection, collector, router, scales, layer + 1, packed
            )
        queries = packed[:, :model_width].reshape(tokens_dev, HEADS, HEAD_DIM)
        key_heads = packed[:, model_width : 2 * model_width].reshape(tokens_dev, HEADS, HEAD_DIM)
        value_heads = packed[:, 2 * model_width :].reshape(tokens_dev, HEADS, HEAD_DIM)
        scores = score_heads(queries, key_heads, bias_heads, same_segment)
        row_peak = jnp.max(scores, axis=-1, keepdims=True)
        log_total = row_peak + jnp.log(jnp.sum(jnp.exp(scores - row_peak), axis=-1, keepdims=True))
        attention = jnp.exp(scores - log_total)
        mixed_heads = jnp.einsum(
            "hts,shd->thd",
            attention.astype(jnp.bfloat16),
            value_heads,
            preferred_element_type=jnp.float32,
        )
        mixed_heads = mixed_heads.reshape(tokens_dev, model_width).astype(jnp.bfloat16)
        middle = residual + jnp.dot(mixed_heads, collect_full, preferred_element_type=jnp.float32)
        normed_two, base_two, scale_two = rms_forward(middle, gain_two)
        router_float = router_full.astype(jnp.float32)
        logits = jnp.dot(normed_two, router_float, precision=HIGHEST)
        gate_probs = jax.nn.softmax(logits, axis=-1)
        gate_value = jnp.sum(gate_probs * route_float, axis=1) * retained
        sent = normed_two.astype(jnp.bfloat16)
        buffer = jnp.dot(slot_back, sent, preferred_element_type=jnp.float32).astype(jnp.bfloat16)
        rows_all = send_rows(buffer.reshape(experts, capacity, model_width))
        hidden_pre = jnp.dot(rows_all, upward[layer, 0], preferred_element_type=jnp.float32)
        hidden_act = jax.nn.gelu(hidden_pre).astype(jnp.bfloat16)
        partial_value = jnp.dot(hidden_act, downward[layer, 0], preferred_element_type=jnp.float32)
        returned = return_rows(partial_value)
        expert_tokens = jnp.dot(slot_hot, returned, preferred_element_type=jnp.float32)
        residual = middle + gate_value[:, None] * expert_tokens
        stored.append(
            dict(
                fetched=fetched,
                base_one=base_one,
                scale_one=scale_one,
                hidden_one=hidden_one,
                queries=queries,
                key_heads=key_heads,
                value_heads=value_heads,
                log_total=log_total,
                mixed_heads=mixed_heads,
                base_two=base_two,
                scale_two=scale_two,
                normed_two=normed_two,
                gate_probs=gate_probs,
                gate_value=gate_value,
                rows_all=rows_all,
                hidden_pre=hidden_pre,
                hidden_act=hidden_act,
                expert_tokens=expert_tokens,
            )
        )
    grad_residual = cotangent.astype(jnp.float32)
    pair_total = jnp.zeros((HEADS, tokens_dev, tokens_dev), jnp.float32)
    proj_grads, collect_grads, up_grads, down_grads = [], [], [], []
    small_rows = []
    for layer in reversed(range(layers)):
        saved_layer = stored[layer]
        proj_full, collect_full, router_full, scales_full = saved_layer["fetched"]
        gain_one = scales_full[:, 0].astype(jnp.float32)
        gain_two = scales_full[:, 1].astype(jnp.float32)
        router_float = router_full.astype(jnp.float32)
        gate_value = saved_layer["gate_value"]
        gate_probs = saved_layer["gate_probs"]
        grad_gate = jnp.sum(grad_residual * saved_layer["expert_tokens"], axis=1)
        grad_tokens_out = (gate_value[:, None] * grad_residual).astype(jnp.bfloat16)
        grad_buffer = jnp.dot(
            slot_back, grad_tokens_out, preferred_element_type=jnp.float32
        ).astype(jnp.bfloat16)
        grad_spread = send_rows(grad_buffer.reshape(experts, capacity, model_width))
        grad_act = jnp.dot(grad_spread, downward[layer, 0].T, preferred_element_type=jnp.float32)
        gelu_value, gelu_pull = jax.vjp(jax.nn.gelu, saved_layer["hidden_pre"])
        grad_pre = gelu_pull(grad_act)[0].astype(jnp.bfloat16)
        grad_down_t = jnp.dot(
            grad_spread.T, saved_layer["hidden_act"], preferred_element_type=jnp.float32
        )
        grad_up = jnp.dot(saved_layer["rows_all"].T, grad_pre, preferred_element_type=jnp.float32)
        grad_sent_part = jnp.dot(grad_pre, upward[layer, 0].T, preferred_element_type=jnp.float32)
        grad_back = return_rows(grad_sent_part)
        grad_normed_two = jnp.dot(slot_hot, grad_back, preferred_element_type=jnp.float32)
        grad_gprobs = (grad_gate * retained)[:, None] * route_float
        grad_logits = gate_probs * (
            grad_gprobs - jnp.sum(grad_gprobs * gate_probs, axis=1, keepdims=True)
        )
        grad_router_t = jnp.dot(grad_logits.T, saved_layer["normed_two"], precision=HIGHEST)
        grad_normed_two = grad_normed_two + jnp.dot(grad_logits, router_float.T, precision=HIGHEST)
        grad_mid_norm, grad_gain_two = rms_backward(
            grad_normed_two, gain_two, saved_layer["base_two"], saved_layer["scale_two"]
        )
        grad_middle = grad_residual + grad_mid_norm
        grad_branch = grad_middle.astype(jnp.bfloat16)
        grad_collect = jnp.dot(
            saved_layer["mixed_heads"].T, grad_branch, preferred_element_type=jnp.float32
        )
        grad_mixed = jnp.dot(
            grad_branch, collect_full.T, preferred_element_type=jnp.float32
        ).astype(jnp.bfloat16)
        grad_mixed = grad_mixed.reshape(tokens_dev, HEADS, HEAD_DIM)
        queries = saved_layer["queries"]
        key_heads = saved_layer["key_heads"]
        value_heads = saved_layer["value_heads"]
        scores = score_heads(queries, key_heads, bias_heads, same_segment)
        attention = jnp.exp(scores - saved_layer["log_total"])
        grad_values = jnp.einsum(
            "hts,thd->shd",
            attention.astype(jnp.bfloat16),
            grad_mixed,
            preferred_element_type=jnp.float32,
        )
        grad_attention = jnp.einsum(
            "thd,shd->hts", grad_mixed, value_heads, preferred_element_type=jnp.float32
        )
        grad_scores = attention * (
            grad_attention - jnp.sum(grad_attention * attention, axis=-1, keepdims=True)
        )
        grad_scores_low = grad_scores.astype(jnp.bfloat16)
        grad_queries = (
            jnp.einsum(
                "hts,shd->thd", grad_scores_low, key_heads, preferred_element_type=jnp.float32
            )
            * head_scale
        )
        grad_keys = (
            jnp.einsum("hts,thd->shd", grad_scores_low, queries, preferred_element_type=jnp.float32)
            * head_scale
        )
        pair_total = pair_total + grad_scores_low.astype(jnp.float32)
        grad_packed = jnp.concatenate(
            [
                grad_queries.reshape(tokens_dev, model_width),
                grad_keys.reshape(tokens_dev, model_width),
                grad_values.reshape(tokens_dev, model_width),
            ],
            axis=1,
        ).astype(jnp.bfloat16)
        grad_proj = jnp.dot(
            saved_layer["hidden_one"].T, grad_packed, preferred_element_type=jnp.float32
        )
        grad_hidden_one = jnp.dot(grad_packed, proj_full.T, preferred_element_type=jnp.float32)
        grad_in_norm, grad_gain_one = rms_backward(
            grad_hidden_one, gain_one, saved_layer["base_one"], saved_layer["scale_one"]
        )
        grad_residual = grad_middle + grad_in_norm
        expert_shares = reduce_experts(grad_up, grad_down_t)
        shares = (reduce_rows(grad_proj), reduce_rows(grad_collect))
        small_rows = [grad_router_t, grad_gain_one[None], grad_gain_two[None]] + small_rows
        proj_grads.insert(0, shares[0])
        collect_grads.insert(0, shares[1])
        up_grads.insert(0, expert_shares[0][None])
        down_grads.insert(0, expert_shares[1].T[None])
    offset_total = pairs_to_offsets(pair_total, tokens_dev)
    table_total = jnp.dot(offset_total, offset_hot, precision=HIGHEST)
    table_rows = jnp.pad(table_total, ((0, 0), (0, model_width - buckets_all)))
    small_sum = sum_everywhere(jnp.concatenate(small_rows + [table_rows]))
    split = layers * (experts + 2)
    table_sum = small_sum[split:, :buckets_all].T
    width = router.shape[1]
    owner = lax.axis_index("shard") * lax.axis_size("dp") + lax.axis_index("dp")
    small_mine = lax.dynamic_slice_in_dim(small_sum[:split], owner * width, width, 1)
    small_mine = jnp.swapaxes(small_mine.reshape(layers, experts + 2, width), 1, 2)
    return (
        residual.astype(jnp.bfloat16),
        grad_residual,
        jnp.stack(proj_grads),
        jnp.stack(collect_grads),
        small_mine[:, :, :experts],
        small_mine[:, :, experts:],
        jnp.stack(up_grads),
        jnp.stack(down_grads),
        table_sum,
    )


def solution(mesh):
    in_specs = (
        P(("expert", "shard", "dp"), None),
        P(("expert", "shard", "dp"), None),
        P(("expert", "shard", "dp"), None),
        P(),
        P(),
        P(None, ("shard", "dp"), None),
        P(None, ("shard", "dp"), None),
        P(None, ("shard", "dp"), None),
        P(None, ("shard", "dp"), None),
        P(None, "expert", None, "shard"),
        P(None, "expert", "shard", None),
        P(("expert", "shard", "dp"), None),
    )
    out_specs = (
        P(("expert", "shard", "dp"), None),
        P(("expert", "shard", "dp"), None),
        P(None, ("shard", "dp"), None),
        P(None, ("shard", "dp"), None),
        P(None, ("shard", "dp"), None),
        P(None, ("shard", "dp"), None),
        P(None, "expert", "dp", "shard"),
        P(None, "expert", "shard", "dp"),
        P(),
    )
    return jax.shard_map(body, mesh=mesh, in_specs=in_specs, out_specs=out_specs, check_vma=False)
```
